256 devices in a mesh: row: 8 (over y, x_lo), col: 32 (over z, x_hi, core).
Axes of the slice: x: 4 (x_hi: 2, x_lo: 2; x = x_hi * 2 + x_lo), y: 4, z: 8, core: 2. Of those that a mesh axis runs over, the one named last changes fastest.
Arguments:
- source_embed: bfloat16 [64, 49152], P(None, ('row', 'col')), may hold values from -0.8984375 to 0.8984375
- target_embed: bfloat16 [64, 49152], P(None, ('row', 'col')), may hold values from -0.8984375 to 0.8984375
- left_factor: bfloat16 [128, 49152], P(None, ('row', 'col')), may hold values from -6 to 6
- right_factor: bfloat16 [128, 49152], P(None, ('row', 'col')), may hold values from -0.01953125 to 0.01953125
Outputs:
- source_grad: float32 [64, 49152], P(None, ('row', 'col'))
- target_grad: float32 [64, 49152], P(None, ('row', 'col'))
The draws below stay inside these ranges and needn't reach their ends.
All inputs are finite; a program needn't handle non-finite values.
Results may differ from the reference program's by a relative error of at most 0.0055.
Values may be sent and summed in bfloat16 or wider, within the bound.
A program may use at most 64 MiB of HBM per device.

```python
import math
import jax
import jax.numpy as jnp
from jax import lax

E = 64
R = 128
FRAMES = 49152


def levels(rng, shape, cuts, low, high):
    def one(position, shards_of):
        steps = jax.random.uniform(jax.random.fold_in(jax.random.fold_in(rng, 6), position), (shards_of,), jnp.float32, low / len(cuts), high / len(cuts))
        return jnp.repeat(jnp.exp(steps), shape[position] // shards_of).reshape((-1,) + (1,) * (len(shape) - position - 1))

    loudness = one(*cuts[0])
    for cut in cuts[1:]:
        loudness = loudness * one(*cut)
    return loudness


def bell_draw(stream_key, dims, width, most, cuts=(), kind=jnp.bfloat16):
    factor_of = levels(stream_key, dims, cuts, -0.22, 0.18) if cuts else 1.0
    drawn = jax.random.normal(stream_key, dims, jnp.float32) * width * factor_of
    return jnp.minimum(jnp.maximum(drawn, -most), most).astype(kind)


def setup_inputs(seed: int = 0) -> dict:
    arg_keys = jax.random.split(jax.random.key(seed), 5)
    source_embed = bell_draw(arg_keys[0], (E, FRAMES), 0.15, 0.8984375, ((1, 256),))
    target_embed = bell_draw(arg_keys[1], (E, FRAMES), 0.15, 0.8984375, ((1, 256),))
    left_factor = bell_draw(arg_keys[2], (R, FRAMES), 1.0, 6.0, ((1, 256),))
    right_factor = bell_draw(arg_keys[3], (R, FRAMES), (R * FRAMES // 64) ** -0.5, 0.01953125, ((1, 256),))
    return dict(source_embed=source_embed, target_embed=target_embed, left_factor=left_factor, right_factor=right_factor)


kernel_rate = 0.5


def tile_terms(rows_embed, rows_factor, cols_embed, cols_factor, cols_square):
    rows_square = jnp.sum(jnp.square(rows_embed.astype(jnp.float32)), axis=0)
    cross = lax.dot_general(rows_embed, cols_embed, (((0,), (0,)), ((), ())), preferred_element_type=jnp.float32)
    distance = rows_square[:, None] + cols_square[None, :] - 2.0 * cross
    kernel = jnp.exp(-kernel_rate * distance)
    adjoint = lax.dot_general(rows_factor, cols_factor, (((0,), (0,)), ((), ())), preferred_element_type=jnp.float32)
    weighted = (adjoint * kernel).astype(jnp.bfloat16)
    weighted_wide = weighted.astype(jnp.float32)
    row_pull = lax.dot_general(cols_embed, weighted, (((1,), (1,)), ((), ())), preferred_element_type=jnp.float32)
    row_mass = jnp.sum(weighted_wide, axis=1)
    col_pull = jnp.dot(rows_embed, weighted, preferred_element_type=jnp.float32)
    col_mass = jnp.sum(weighted_wide, axis=0)
    return row_pull, row_mass, col_pull, col_mass


def reference(source_embed, target_embed, left_factor, right_factor):
    embed_width = source_embed.shape[0]
    frames = source_embed.shape[1]
    block_rows = math.gcd(frames, 1024)
    steps_count = frames // block_rows
    target_square = jnp.sum(jnp.square(target_embed.astype(jnp.float32)), axis=0)

    def visit_block(totals, counter):
        begin_at = (counter * block_rows).astype(jnp.int32)
        rows_embed = lax.dynamic_slice_in_dim(source_embed, begin_at, block_rows, 1)
        rows_factor = lax.dynamic_slice_in_dim(left_factor, begin_at, block_rows, 1)
        row_pull, row_mass, col_pull, col_mass = tile_terms(rows_embed, rows_factor, target_embed, right_factor, target_square)
        row_grad = -2.0 * kernel_rate * (row_mass[None, :] * rows_embed.astype(jnp.float32) - row_pull)
        return (totals[0] + col_pull, totals[1] + col_mass), row_grad

    start_totals = (jnp.zeros((embed_width, frames), jnp.float32), jnp.zeros((frames,), jnp.float32))
    totals, row_grads = lax.scan(visit_block, start_totals, jnp.arange(steps_count, dtype=jnp.int32))
    source_grad = jnp.transpose(row_grads, (1, 0, 2)).reshape(embed_width, frames)
    target_grad = 2.0 * kernel_rate * (totals[0] - totals[1][None, :] * target_embed.astype(jnp.float32))
    return source_grad, target_grad
```

```python
import functools

import jax
import jax.numpy as jnp
from jax import lax
from jax.experimental import pallas as pl
from jax.experimental.pallas import tpu as pltpu
from jax.sharding import PartitionSpec as P

MESH = pl.DeviceIdType.MESH
f32, bf16 = jnp.float32, jnp.bfloat16

E = 64
R = 128
B = 192
LANES = E + 64 + R
GROUP = 16
CHUNK = 4 * B
ONE_X, ONE_Y = E + 3, E

PLANE = [(0, 0), (1, 0), (3, 0), (0, 1), (0, 3), (1, 1), (3, 3), (1, 3), (3, 1), (2, 0), (0, 2), (2, 1), (2, 3), (1, 2), (3, 2), (2, 2)]
LINE = [(0, 0), (0, 1), (1, 0), (7, 0), (1, 1), (7, 1), (2, 0), (6, 0), (2, 1), (6, 1), (3, 0), (5, 0), (3, 1), (5, 1), (4, 0), (4, 1)]

ORDER = [(0, 0), (0, 1), (1, 0), (1, 1), (0, 2), (1, 2), (2, 0), (2, 1), (2, 2), (0, 3), (1, 3), (2, 3), (3, 0), (3, 1), (3, 2), (3, 3)]

NN = (((1,), (0,)), ((), ()))
NT = (((1,), (1,)), ((), ()))


def dot(a, b, dims):
    return lax.dot_general(a, b, dims, preferred_element_type=f32)


def prepare(embed_ref, factor_ref, first, rows_ref, stack):
    wide = embed_ref[...].astype(f32)
    half = -0.5 * jnp.sum(wide * wide, axis=0, keepdims=True)
    high = half.astype(bf16).astype(f32)
    middle = (half - high).astype(bf16).astype(f32)
    low = half - high - middle
    place = lax.broadcasted_iota(jnp.int32, (E, B), 0)
    norms, ones = (0, 3) if first else (3, 0)
    extra = jnp.where((place >= ones) & (place < ones + 3), 1.0, 0.0)
    for at, piece in enumerate((high, middle, low)):
        extra = jnp.where(place == norms + at, piece, extra)
    stack[0:E, :] = embed_ref[...]
    stack[E : 2 * E, :] = extra.astype(bf16)
    stack[2 * E : LANES, :] = factor_ref[...]
    down = lax.broadcasted_iota(jnp.int32, (B, B), 0)
    along = lax.broadcasted_iota(jnp.int32, (B, B), 1)
    unit = jnp.where(down == along, 1.0, 0.0).astype(bf16)
    rows_ref[0:B, :] = dot(unit, stack[...], NT).astype(bf16)


def pack(block):
    lane = lax.broadcasted_iota(jnp.int32, (B // 2, 128), 1)
    return jnp.where(lane < E, block[0 : B // 2], pltpu.roll(block[B // 2 :], E, 1)).astype(bf16)


def unpack(total, out_ref):
    tall = jnp.concatenate([total, jnp.zeros((128 - B // 2, 128), f32)], axis=0).T
    lane = lax.broadcasted_iota(jnp.int32, (E, 128), 1)
    later = pltpu.roll(tall[E:, :], B // 2, 1)
    out_ref[:, 0:128] = jnp.where(lane < B // 2, tall[0:E, :], later)
    out_ref[:, 128:B] = later[:, 0 : B - 128]


def kernel(source, target, left, right, out_s, out_t, xa, ya, xt, rp, cp, stack, send_r, send_c, recv_r, recv_c, *sems):
    gx_s, gx_r, gy_s, gy_r, rr_s, rr_r, rc_s, rc_r = sems
    row, col = lax.axis_index("row"), lax.axis_index("col")
    y, z, core = row // 2, col // 4, col % 2
    x = (col // 2) % 2 * 2 + row % 2

    def device(x, y, z, core):
        return (y * 2 + x % 2, (z * 2 + x // 2) * 2 + core)

    plane = [device((x + dx) % 4, (y + dy) % 4, z, core) for dx, dy in PLANE]
    line = [device(x, y, (z + dz) % 8, (core + dc) % 2) for dz, dc in LINE]
    plane_owner = [device((x + 4 - dx) % 4, (y + 4 - dy) % 4, z, core) for dx, dy in PLANE]
    line_owner = [device(x, y, (z + 8 - dz) % 8, (core + 2 - dc) % 2) for dz, dc in LINE]

    def copy(src, dst, send, recv, peer):
        return pltpu.make_async_remote_copy(
            src_ref=src, dst_ref=dst, send_sem=send, recv_sem=recv, device_id=peer, device_id_type=MESH
        )

    def gather_x(k):
        return copy(xa.at[pl.ds(0, B), :], xa.at[pl.ds(k * B, B), :], gx_s.at[k], gx_r.at[k], plane[k])

    def gather_y(k):
        return copy(ya.at[pl.ds(0, B), :], ya.at[pl.ds(k * B, B), :], gy_s.at[k], gy_r.at[k], line[k])

    def give_r(k):
        return copy(send_r.at[k], recv_r.at[k], rr_s.at[k], rr_r.at[k], plane_owner[k])

    def give_c(k):
        return copy(send_c.at[k], recv_c.at[k], rc_s.at[k], rc_r.at[k], line_owner[k])

    barrier = pltpu.get_barrier_semaphore()
    for k in range(1, GROUP):
        pl.semaphore_signal(barrier, inc=1, device_id=plane[k], device_id_type=MESH)
        pl.semaphore_signal(barrier, inc=1, device_id=line[k], device_id_type=MESH)
    prepare(source, left, True, xa, stack)
    prepare(target, right, False, ya, stack)
    pl.semaphore_wait(barrier, 2 * (GROUP - 1))
    for k in range(1, GROUP):
        gather_x(k).start()
        gather_y(k).start()
    rp[...] = jnp.zeros_like(rp)
    cp[...] = jnp.zeros_like(cp)

    def arrive_x(chunk):
        for k in range(max(4 * chunk, 1), 4 * chunk + 4):
            gather_x(k).wait_recv()
        rows = slice(chunk * CHUNK, (chunk + 1) * CHUNK)
        xt[:, rows] = xa[rows, 0:128].T

    def arrive_y(chunk):
        for k in range(max(4 * chunk, 1), 4 * chunk + 4):
            gather_y(k).wait_recv()

    def finish(pulls, mass, embeds, chunk, send, recv, give):
        grads = pulls - pulls[:, mass : mass + 1] * embeds.astype(f32)
        for i in range(4):
            k = 4 * chunk + i
            packed = pack(grads[i * B : (i + 1) * B])
            if k == 0:
                recv[0] = packed
            else:
                send[k] = packed
                give(k).start()

    def tile(t, _):
        rb = sum(jnp.where(t == i, r, 0) for i, (r, _) in enumerate(ORDER))
        cb = sum(jnp.where(t == i, c, 0) for i, (_, c) in enumerate(ORDER))
        for i, (r, c) in enumerate(ORDER):
            new_x = all(r != a for a, _ in ORDER[:i])
            new_y = all(c != a for _, a in ORDER[:i])
            if new_x or new_y:

                @pl.when(t == i)
                def _():
                    if new_x:
                        arrive_x(r)
                    if new_y:
                        arrive_y(c)

        rows = pl.ds(pl.multiple_of(rb * CHUNK, CHUNK), CHUNK)
        cols = pl.ds(pl.multiple_of(cb * CHUNK, CHUNK), CHUNK)
        arg = dot(xa[rows, 0:128], ya[cols, 0:128], NT)
        adjoint = dot(xa[rows, 128:256], ya[cols, 128:256], NT)
        weighted = (adjoint * jnp.exp(arg)).astype(bf16)
        rp[rows, :] += dot(weighted, ya[cols, 0:128], NN)
        cp[0:80, cols] += dot(xt[0:80, rows], weighted, NN)

        for i, (r, c) in enumerate(ORDER):
            last_x = all(r != a for a, _ in ORDER[i + 1 :])
            last_y = all(c != a for _, a in ORDER[i + 1 :])
            if last_x or last_y:

                @pl.when(t == i)
                def _():
                    if last_x:
                        at = slice(r * CHUNK, (r + 1) * CHUNK)
                        finish(rp[at, :], ONE_Y, xa[at, 0:128], r, send_r, recv_r, give_r)
                    if last_y:
                        at = slice(c * CHUNK, (c + 1) * CHUNK)
                        finish(cp[:, at].T, ONE_X, ya[at, 0:128], c, send_c, recv_c, give_c)

        return 0

    lax.fori_loop(0, len(ORDER), tile, 0)

    for recv, give, out in ((recv_r, give_r, out_s), (recv_c, give_c, out_t)):
        total = recv[0].astype(f32)
        for k in range(1, GROUP):
            give(k).wait_recv()
            total = total + recv[k].astype(f32)
        unpack(total, out)
    for k in range(1, GROUP):
        for each in (gather_x, gather_y, give_r, give_c):
            each(k).wait_send()


def per_device(source_embed, target_embed, left_factor, right_factor):
    frames = GROUP * B
    vmem = pl.BlockSpec(memory_space=pltpu.VMEM)
    return pl.pallas_call(
        kernel,
        out_shape=(jax.ShapeDtypeStruct((E, B), f32),) * 2,
        in_specs=[vmem] * 4,
        out_specs=(vmem,) * 2,
        scratch_shapes=[
            pltpu.VMEM((frames, LANES), bf16),
            pltpu.VMEM((frames, LANES), bf16),
            pltpu.VMEM((128, frames), bf16),
            pltpu.VMEM((frames, 128), f32),
            pltpu.VMEM((128, frames), f32),
            pltpu.VMEM((LANES, B), bf16),
        ]
        + [pltpu.VMEM((GROUP, B // 2, 128), bf16)] * 4
        + [pltpu.SemaphoreType.DMA((GROUP,))] * 8,
        compiler_params=pltpu.CompilerParams(
            collective_id=0, has_side_effects=True, vmem_limit_bytes=48 << 20
        ),
        cost_estimate=pl.CostEstimate(
            flops=2 * frames * frames * (2 * E + 2 * E + R), bytes_accessed=1 << 18, transcendentals=frames * frames
        ),
    )(source_embed, target_embed, left_factor, right_factor)


def solution(mesh):
    spec = P(None, ("row", "col"))
    return jax.shard_map(
        per_device, mesh=mesh, in_specs=(spec,) * 4, out_specs=(spec,) * 2, check_vma=False
    )
```

```python
import functools

import jax
import jax.numpy as jnp
from jax import lax
from jax.experimental import pallas as pl
from jax.experimental.pallas import tpu as pltpu
from jax.sharding import PartitionSpec as P

MESH = pl.DeviceIdType.MESH
f32, bf16 = jnp.float32, jnp.bfloat16

E = 64
R = 128
B = 192
LANES = E + 64 + R
GROUP = 16
CHUNK = 4 * B
H = B // 2
ONE_X, ONE_Y = E + 3, E

RING = [0, 1, 3, 2]
LINE = [0, 1, 7, 2, 6, 3, 5, 4]

ORDER = [(0, 0), (0, 1), (2, 0), (2, 1), (0, 2), (2, 2), (1, 2), (1, 1), (0, 3), (2, 3), (1, 3), (3, 3), (3, 2), (3, 1), (3, 0), (1, 0)]
PASS_ON = {
    0: [(1, 0), (2, 0), (1, 1), (2, 1)],
    1: [(3, 0), (4, 0), (3, 1), (4, 1)],
    2: [(5, 0), (6, 1), (5, 1), (6, 0)],
    5: [(7, 0), (7, 1)],
}

NN = (((1,), (0,)), ((), ()))
NT = (((1,), (1,)), ((), ()))


def dot(a, b, dims):
    return lax.dot_general(a, b, dims, preferred_element_type=f32)


def prepare(embed_ref, factor_ref, first, rows_ref, places, stack):
    wide = embed_ref[...].astype(f32)
    half = -0.5 * jnp.sum(wide * wide, axis=0, keepdims=True)
    high = half.astype(bf16).astype(f32)
    middle = (half - high).astype(bf16).astype(f32)
    low = half - high - middle
    place = lax.broadcasted_iota(jnp.int32, (E, B), 0)
    norms, ones = (0, 3) if first else (3, 0)
    extra = jnp.where((place >= ones) & (place < ones + 3), 1.0, 0.0)
    for at, piece in enumerate((high, middle, low)):
        extra = jnp.where(place == norms + at, piece, extra)
    stack[0:E, :] = embed_ref[...]
    stack[E : 2 * E, :] = extra.astype(bf16)
    down = lax.broadcasted_iota(jnp.int32, (B, B), 0)
    along = lax.broadcasted_iota(jnp.int32, (B, B), 1)
    unit = jnp.where(down == along, 1.0, 0.0).astype(bf16)
    left_lanes = dot(unit, stack[...], NT).astype(bf16)
    for half, at in enumerate(places):
        rows_ref[at : at + H, 0 : 2 * E] = left_lanes[half * H : (half + 1) * H]
        rows_ref[at : at + H, 2 * E : LANES] = factor_ref[half * H : (half + 1) * H, :]


def pack(block):
    n = block.shape[0] // 2
    lane = lax.broadcasted_iota(jnp.int32, (n, 128), 1)
    return jnp.where(lane < E, block[0:n], pltpu.roll(block[n:], E, 1)).astype(bf16)


def unpack(total, runs, out_ref):
    tall = jnp.concatenate([total, jnp.zeros((128 - H, 128), f32)], axis=0).T
    size = B // len(runs)
    lane = lax.broadcasted_iota(jnp.int32, (E, 128), 1)
    for begin in (0, 128):
        piece = jnp.zeros((E, 128), f32)
        for at, row, half in runs:
            if at < begin + 128 and at + size > begin:
                moved = pltpu.roll(tall[half * E : (half + 1) * E, :], (at - begin - row) % 128, 1)
                inside = (lane >= at - begin) & (lane < at - begin + size)
                piece = jnp.where(inside, moved, piece)
        width = min(128, B - begin)
        out_ref[:, begin : begin + width] = piece[:, 0:width]


def kernel(source, target, left, right, out_s, out_t, xa, ya, xt, rp, cp, stack, own, send_r, recv_r, mine, theirs, given, send_c, recv_c, *sems):
    in_sems, gx_s, gx_r, gz_s, gz_r, gc_s, gc_r, rr_s, rr_r, rc_s, rc_r, rz_s, rz_r = sems
    row, col = lax.axis_index("row"), lax.axis_index("col")
    y, z, core = row // 2, col // 4, col % 2
    x = (col // 2) % 2 * 2 + row % 2
    own_embed, own_factor = own

    def device(x, y, z, core):
        return (y % 4 * 2 + x % 2, (z % 8 * 2 + x % 4 // 2) * 2 + core)

    def frames_of(h, k, i, sign):
        dx, dy = (RING[i], RING[k]) if h == 0 else (RING[k], RING[i])
        return device(x + sign * dx % 4, y + sign * dy % 4, z, core)

    line_owner = [device(x, y, z + 8 - dz, core) for dz in LINE]
    up, down, sibling = device(x, y, z + 1, core), device(x, y, z + 7, core), device(x, y, z, 1 - core)

    def copy(src, dst, send, recv, peer):
        return pltpu.make_async_remote_copy(
            src_ref=src, dst_ref=dst, send_sem=send, recv_sem=recv, device_id=peer, device_id_type=MESH
        )

    def place(h, k, i):
        return (8 * k + 4 * h + i) * H

    def first_step(h, i):
        sem = 4 * h + i
        peer = frames_of(h, 0, i, 1)
        return copy(xa.at[pl.ds(place(h, 0, 0), H), :], xa.at[pl.ds(place(h, 0, i), H), :], gx_s.at[sem], gx_r.at[sem], peer)

    def second_step(h, k):
        sem = 8 + 4 * h + k
        peer = frames_of(h, k, 0, 1)
        return copy(xa.at[pl.ds(place(h, 0, 0), 4 * H), :], xa.at[pl.ds(place(h, k, 0), 4 * H), :], gx_s.at[sem], gx_r.at[sem], peer)

    def hop(p, half):
        before = {1: 0, 2: 0, 3: 1, 4: 2, 5: 3, 6: 4, 7: 5 + half}[p]
        at, old = 2 * p * B + half * H, 2 * before * B + half * H
        peer = up if before % 2 and p > 2 or p == 1 else down
        return copy(ya.at[pl.ds(old, H), :], ya.at[pl.ds(at, H), :], gz_s.at[2 * p + half], gz_r.at[2 * p + half], peer)

    def share(p):
        return copy(ya.at[pl.ds(2 * p * B, B), :], ya.at[pl.ds((2 * p + 1) * B, B), :], gc_s.at[p], gc_r.at[p], sibling)

    def give_r(h, k, i):
        slot = 8 * k + 4 * h + i
        return copy(send_r.at[slot], recv_r.at[slot], rr_s.at[slot], rr_r.at[slot], frames_of(h, k, i, -1))

    def give_pair(p):
        return copy(given.at[p], theirs.at[p], rc_s.at[p], rc_r.at[p], sibling)

    def give_z(p):
        return copy(send_c.at[p], recv_c.at[p], rz_s.at[p], rz_r.at[p], line_owner[p])

    blocks = [(h, k, i) for k in range(4) for h in range(2) for i in range(4) if k or i]
    reads = [
        pltpu.make_async_copy(src, dst, in_sems.at[n])
        for n, (src, dst) in enumerate(zip((target, right, source, left), (own_embed.at[0], own_factor.at[0], own_embed.at[1], own_factor.at[1])))
    ]
    for read in reads:
        read.start()
    barrier = pltpu.get_barrier_semaphore()
    greet = [frames_of(0, k, i, 1) for h, k, i in blocks if h == 0] + line_owner[1:] + [sibling]
    for peer in greet:
        pl.semaphore_signal(barrier, inc=1, device_id=peer, device_id_type=MESH)
    for read in reads:
        read.wait()
    prepare(own_embed.at[0], own_factor.at[0], False, ya, (0, H), stack)
    prepare(own_embed.at[1], own_factor.at[1], True, xa, (place(0, 0, 0), place(1, 0, 0)), stack)
    pl.semaphore_wait(barrier, len(greet))
    for half in range(2):
        hop(1, half).start()
        hop(2, half).start()
    for i in range(1, 4):
        for h in range(2):
            first_step(h, i).start()
    share(0).start()
    rp[...] = jnp.zeros_like(rp)
    cp[...] = jnp.zeros_like(cp)

    def arrive_x(chunk):
        for h in range(2):
            if chunk == 0:
                for i in range(1, 4):
                    first_step(h, i).wait_recv()
                for k in range(1, 4):
                    second_step(h, k).start()
            else:
                second_step(h, chunk).wait_recv()
        rows = slice(chunk * CHUNK, (chunk + 1) * CHUNK)
        xt[:, rows] = xa[rows, 0:128].T

    def pass_on(p, half):
        hop(p, half).wait_recv()
        if p < 5:
            hop(p + 2, half).start()
        elif p == 5 + half:
            hop(7, half).start()
        if half == last_half[p]:
            share(p).start()

    last_half = {p: half for at in sorted(PASS_ON) for p, half in PASS_ON[at]}

    def arrive_y(chunk):
        for p in (2 * chunk, 2 * chunk + 1):
            share(p).wait_recv()

    def grads(pulls, mass, embeds):
        return pulls - pulls[:, mass : mass + 1] * embeds.astype(f32)

    def finish_rows(chunk):
        at = slice(chunk * CHUNK, (chunk + 1) * CHUNK)
        part = grads(rp[at, :], ONE_Y, xa[at, 0:128])
        for h in range(2):
            for i in range(4):
                n = 4 * h + i
                slot = 8 * chunk + n
                packed = pack(part[n * H : (n + 1) * H])
                if chunk == 0 and i == 0:
                    recv_r[slot] = packed
                else:
                    send_r[slot] = packed
                    give_r(h, chunk, i).start()

    def finish_cols(chunk):
        at = slice(chunk * CHUNK, (chunk + 1) * CHUNK)
        part = grads(cp[:, at].T, ONE_X, ya[at, 0:128])
        for i in range(2):
            p = 2 * chunk + i
            given[p] = pack(part[(2 * i + 1) * B : (2 * i + 2) * B])
            give_pair(p).start()
            mine[p] = pack(part[2 * i * B : (2 * i + 1) * B])

    def combine_cols(chunk):
        for p in (2 * chunk, 2 * chunk + 1):
            give_pair(p).wait_recv()
            both = (mine[p].astype(f32) + theirs[p].astype(f32)).astype(bf16)
            if p == 0:
                recv_c[0] = both
            else:
                send_c[p] = both
                give_z(p).start()

    firsts = {}
    for i, (r, c) in enumerate(ORDER):
        if i in PASS_ON:
            firsts.setdefault(i, []).extend(functools.partial(pass_on, p, half) for p, half in PASS_ON[i])
        if all(c != a for _, a in ORDER[:i]):
            firsts.setdefault(i, []).append(functools.partial(arrive_y, c))
        if all(r != a for a, _ in ORDER[:i]):
            firsts.setdefault(i, []).append(functools.partial(arrive_x, r))
    lasts = {}
    for i, (r, c) in enumerate(ORDER):
        if all(c != a for _, a in ORDER[i + 1 :]):
            lasts.setdefault(i, []).append(functools.partial(finish_cols, c))
            lasts.setdefault(min(i + 1, len(ORDER) - 1), []).append(functools.partial(combine_cols, c))
        if all(r != a for a, _ in ORDER[i + 1 :]):
            lasts.setdefault(i, []).append(functools.partial(finish_rows, r))

    last = len(ORDER) - 1
    lasts[last] = sorted(lasts[last], key=lambda f: f.func is combine_cols)

    def at_tile(t, table):
        for i, steps in table.items():

            @pl.when(t == i)
            def _():
                for step in steps:
                    step()

    def tile(t, _):
        rb = sum(jnp.where(t == i, r, 0) for i, (r, _) in enumerate(ORDER))
        cb = sum(jnp.where(t == i, c, 0) for i, (_, c) in enumerate(ORDER))
        at_tile(t, firsts)
        rows = pl.ds(pl.multiple_of(rb * CHUNK, CHUNK), CHUNK)
        cols = pl.ds(pl.multiple_of(cb * CHUNK, CHUNK), CHUNK)
        arg = dot(xa[rows, 0:128], ya[cols, 0:128], NT)
        adjoint = dot(xa[rows, 128:256], ya[cols, 128:256], NT)
        weighted = (adjoint * jnp.exp(arg)).astype(bf16)
        rp[rows, :] += dot(weighted, ya[cols, 0:128], NN)
        cp[0:80, cols] += dot(xt[0:80, rows], weighted, NN)
        at_tile(t, lasts)
        return 0

    lax.fori_loop(0, len(ORDER), tile, 0)

    for h, k, i in blocks:
        give_r(h, k, i).wait_recv()
    halves = []
    for h in range(2):
        slots = [8 * k + 4 * h + i for k in range(4) for i in range(4)]
        halves.append(sum(recv_r[slot].astype(f32) for slot in slots))
    quarter = H // 2
    unpack(jnp.concatenate(halves, axis=0), [(0, 0, 0), (quarter, 0, 1), (H, quarter, 0), (H + quarter, quarter, 1)], out_s)
    for p in range(1, GROUP // 2):
        give_z(p).wait_recv()
    unpack(sum(recv_c[p].astype(f32) for p in range(GROUP // 2)), [(0, 0, 0), (H, 0, 1)], out_t)
    for h, k, i in blocks:
        give_r(h, k, i).wait_send()
        if k == 0:
            first_step(h, i).wait_send()
        elif i == 0:
            second_step(h, k).wait_send()
    for p in range(GROUP // 2):
        share(p).wait_send()
        give_pair(p).wait_send()
        if p > 0:
            give_z(p).wait_send()
            hop(p, 0).wait_send()
            hop(p, 1).wait_send()


def per_device(source_embed, target_embed, left_factor, right_factor):
    frames = GROUP * B
    vmem = pl.BlockSpec(memory_space=pltpu.VMEM)
    return pl.pallas_call(
        kernel,
        out_shape=(jax.ShapeDtypeStruct((E, B), f32),) * 2,
        in_specs=[pl.BlockSpec(memory_space=pl.ANY)] * 4,
        out_specs=(vmem,) * 2,
        scratch_shapes=[
            pltpu.VMEM((frames, LANES), bf16),
            pltpu.VMEM((frames, LANES), bf16),
            pltpu.VMEM((128, frames), bf16),
            pltpu.VMEM((frames, 128), f32),
            pltpu.VMEM((128, frames), f32),
            pltpu.VMEM((2 * E, B), bf16),
            [pltpu.VMEM((2, E, B), bf16), pltpu.VMEM((2, B, R), bf16)],
        ]
        + [pltpu.VMEM((2 * GROUP, H // 2, 128), bf16)] * 2
        + [pltpu.VMEM((GROUP // 2, H, 128), bf16)] * 5
        + [pltpu.SemaphoreType.DMA((4,))]
        + [pltpu.SemaphoreType.DMA((GROUP,))] * 6
        + [pltpu.SemaphoreType.DMA((2 * GROUP,))] * 2
        + [pltpu.SemaphoreType.DMA((GROUP,))] * 4,
        compiler_params=pltpu.CompilerParams(
            collective_id=0, has_side_effects=True, vmem_limit_bytes=60 << 20
        ),
        cost_estimate=pl.CostEstimate(
            flops=2 * frames * frames * (2 * E + 2 * E + R), bytes_accessed=1 << 18, transcendentals=frames * frames
        ),
    )(source_embed, target_embed, left_factor.T, right_factor.T)


def solution(mesh):
    spec = P(None, ("row", "col"))
    return jax.shard_map(
        per_device, mesh=mesh, in_specs=(spec,) * 4, out_specs=(spec,) * 2, check_vma=False
    )
```

```python
import functools

import jax
import jax.numpy as jnp
from jax import lax
from jax.experimental import pallas as pl
from jax.experimental.pallas import tpu as pltpu
from jax.sharding import PartitionSpec as P

MESH = pl.DeviceIdType.MESH
f32, bf16 = jnp.float32, jnp.bfloat16

E = 64
R = 128
B = 192
LANES = E + 64 + R
GROUP = 16
H = B // 2
ONE_X, ONE_Y = E + 3, E

RING = [0, 1, 3, 2]
SLOTS = [(h, 0, i) for h in range(2) for i in range(4)] + [(h, k, 0) for h in range(2) for k in (1, 2)]
SLOTS += [(h, k, i) for h in range(2) for k in (1, 2) for i in (1, 2, 3)] + [(h, 3, i) for h in range(2) for i in range(4)]
LINE = [0, 1, 7, 2, 6, 3, 5, 4]

ROWS = [(0, 1024), (1024, 2304), (2304, 3072)]
COLS = [(0, 1024), (1024, 1792), (1792, 3072)]
TILES = [(0, 0), (0, 1), (1, 0), (1, 1), (0, 2), (1, 2), (2, 2), (2, 1), (2, 0)]

NN = (((1,), (0,)), ((), ()))
NT = (((1,), (1,)), ((), ()))


def dot(a, b, dims):
    return lax.dot_general(a, b, dims, preferred_element_type=f32)


def prepare(embed_ref, factor_ref, first, rows_ref, places, stack):
    wide = embed_ref[...].astype(f32)
    half = -0.5 * jnp.sum(wide * wide, axis=0, keepdims=True)
    high = half.astype(bf16).astype(f32)
    middle = (half - high).astype(bf16).astype(f32)
    low = half - high - middle
    place = lax.broadcasted_iota(jnp.int32, (E, B), 0)
    norms, ones = (0, 3) if first else (3, 0)
    extra = jnp.where((place >= ones) & (place < ones + 3), 1.0, 0.0)
    for at, piece in enumerate((high, middle, low)):
        extra = jnp.where(place == norms + at, piece, extra)
    stack[0:E, :] = embed_ref[...]
    stack[E : 2 * E, :] = extra.astype(bf16)
    down = lax.broadcasted_iota(jnp.int32, (B, B), 0)
    along = lax.broadcasted_iota(jnp.int32, (B, B), 1)
    unit = jnp.where(down == along, 1.0, 0.0).astype(bf16)
    left_lanes = dot(unit, stack[...], NT).astype(bf16)
    for half, at in enumerate(places):
        rows_ref[at : at + H, 0 : 2 * E] = left_lanes[half * H : (half + 1) * H]
        rows_ref[at : at + H, 2 * E : LANES] = factor_ref[half * H : (half + 1) * H, :]


def pack(block):
    n = block.shape[0] // 2
    lane = lax.broadcasted_iota(jnp.int32, (n, 128), 1)
    return jnp.where(lane < E, block[0:n], pltpu.roll(block[n:], E, 1)).astype(bf16)


def unpack(total, runs, out_ref):
    tall = jnp.concatenate([total, jnp.zeros((128 - H, 128), f32)], axis=0).T
    size = B // len(runs)
    lane = lax.broadcasted_iota(jnp.int32, (E, 128), 1)
    for begin in (0, 128):
        piece = jnp.zeros((E, 128), f32)
        for at, row, half in runs:
            if at < begin + 128 and at + size > begin:
                moved = pltpu.roll(tall[half * E : (half + 1) * E, :], (at - begin - row) % 128, 1)
                inside = (lane >= at - begin) & (lane < at - begin + size)
                piece = jnp.where(inside, moved, piece)
        width = min(128, B - begin)
        out_ref[:, begin : begin + width] = piece[:, 0:width]


def kernel(source, target, left, right, out_s, out_t, xa, ya, xt, rp, cp, stack, own, send_r, recv_r, mine, theirs, given, send_c, recv_c, *sems):
    in_sems, gx_s, gx_r, gz_s, gz_r, gc_s, gc_r, rr_s, rr_r, rc_s, rc_r, rz_s, rz_r = sems
    row, col = lax.axis_index("row"), lax.axis_index("col")
    y, z, core = row // 2, col // 4, col % 2
    x = (col // 2) % 2 * 2 + row % 2
    own_embed, own_factor = own

    def device(x, y, z, core):
        return (y % 4 * 2 + x % 2, (z % 8 * 2 + x % 4 // 2) * 2 + core)

    def frames_of(h, k, i, sign):
        dx, dy = (RING[i], RING[k]) if h == 0 else (RING[k], RING[i])
        return device(x + sign * dx % 4, y + sign * dy % 4, z, core)

    line_owner = [device(x, y, z + 8 - dz, core) for dz in LINE]
    line_to = [device(x, y, z + dz, core) for dz in LINE]
    sibling = device(x, y, z, 1 - core)

    def copy(src, dst, send, recv, peer):
        return pltpu.make_async_remote_copy(
            src_ref=src, dst_ref=dst, send_sem=send, recv_sem=recv, device_id=peer, device_id_type=MESH
        )

    def place(h, k, i):
        return SLOTS.index((h, k, i)) * H

    def step_x(h, k, i, n=1):
        old = place(h, 0, i) if k else place(h, 0, 0)
        at = SLOTS.index((h, k, i))
        peer = frames_of(h, k, 0, 1) if k else frames_of(h, 0, i, 1)
        return copy(xa.at[pl.ds(old, n * H), :], xa.at[pl.ds(at * H, n * H), :], gx_s.at[at], gx_r.at[at], peer)

    def hop(p, half=None):
        if p < 5:
            old, at, size, peer = 0, 2 * p * B, B, line_to[p]
        elif p < 7:
            old, at, size, peer = 2 * (p - 2) * B, 2 * p * B, B, line_to[p - 4]
        else:
            off = half * H
            old, at, size, peer = 2 * (3 + half) * B + off, 2 * p * B + off, H, line_to[3 + half]
        sem = p + (half or 0)
        return copy(ya.at[pl.ds(old, size), :], ya.at[pl.ds(at, size), :], gz_s.at[sem], gz_r.at[sem], peer)

    def share(p):
        return copy(ya.at[pl.ds(2 * p * B, B), :], ya.at[pl.ds((2 * p + 1) * B, B), :], gc_s.at[p], gc_r.at[p], sibling)

    def give_r(h, k, i):
        slot = SLOTS.index((h, k, i))
        return copy(send_r.at[slot], recv_r.at[slot], rr_s.at[slot], rr_r.at[slot], frames_of(h, k, i, -1))

    def give_pair(p):
        return copy(given.at[p], theirs.at[p], rc_s.at[p], rc_r.at[p], sibling)

    def give_z(p):
        return copy(send_c.at[p], recv_c.at[p], rz_s.at[p], rz_r.at[p], line_owner[p])

    blocks = [block for block in SLOTS if block[1] or block[2]]
    near = [(h, 0, i) for i in range(1, 4) for h in range(2)] + [(h, k, 0) for h in range(2) for k in (1, 2)]
    later = [(h, k, 1, 3) for k in (1, 2) for h in range(2)]
    far = [(h, 3, 0, 4) for h in range(2)]
    reads = [
        pltpu.make_async_copy(src, dst, in_sems.at[n])
        for n, (src, dst) in enumerate(zip((target, right, source, left), (own_embed.at[0], own_factor.at[0], own_embed.at[1], own_factor.at[1])))
    ]
    for read in reads:
        read.start()
    barrier = pltpu.get_barrier_semaphore()
    greet = [frames_of(0, k, i, 1) for h, k, i in blocks if h == 0] + line_owner[1:] + [sibling]
    for peer in greet:
        pl.semaphore_signal(barrier, inc=1, device_id=peer, device_id_type=MESH)
    for read in reads:
        read.wait()
    prepare(own_embed.at[0], own_factor.at[0], False, ya, (0, H), stack)
    prepare(own_embed.at[1], own_factor.at[1], True, xa, (place(0, 0, 0), place(1, 0, 0)), stack)
    pl.semaphore_wait(barrier, len(greet))
    for p in (1, 2):
        hop(p).start()
    for block in near:
        step_x(*block).start()
    for p in (3, 4):
        hop(p).start()
    share(0).start()
    cp[80:128, :] = jnp.zeros((48, cp.shape[1]), f32)

    def arrive_x(blocks, begin, end):
        for block in blocks:
            step_x(*block).wait_recv()
        xt[:, begin:end] = xa[begin:end, 0:128].T

    def send_later():
        for steps in later:
            step_x(*steps).start()

    def send_far():
        for steps in far:
            step_x(*steps).start()

    def arrive_z(p):
        if p < 7:
            hop(p).wait_recv()
        else:
            hop(7, 0).wait_recv()
            hop(7, 1).wait_recv()
        if p in (3, 4):
            hop(p + 2).start()
            hop(7, p - 3).start()
        share(p).start()

    def arrive_y(*pairs):
        for p in pairs:
            share(p).wait_recv()

    def grads(pulls, mass, embeds):
        return pulls - pulls[:, mass : mass + 1] * embeds.astype(f32)

    def finish_rows(begin, end):
        at = slice(begin * H, end * H)
        part = grads(rp[at, :], ONE_Y, xa[at, 0:128])
        for slot in range(begin, end):
            packed = pack(part[(slot - begin) * H : (slot - begin + 1) * H])
            if SLOTS[slot] in blocks:
                send_r[slot] = packed
                give_r(*SLOTS[slot]).start()
            else:
                recv_r[slot] = packed

    def finish_cols(*pairs):
        begin, end = 2 * pairs[0] * B, 2 * (pairs[-1] + 1) * B
        part = grads(cp[:, begin:end].T, ONE_X, ya[begin:end, 0:128])
        for i, p in enumerate(pairs):
            given[p] = pack(part[(2 * i + 1) * B : (2 * i + 2) * B])
            give_pair(p).start()
            mine[p] = pack(part[2 * i * B : (2 * i + 1) * B])

    def combine_cols(*pairs):
        for p in pairs:
            give_pair(p).wait_recv()
            both = (mine[p].astype(f32) + theirs[p].astype(f32)).astype(bf16)
            if p == 0:
                recv_c[0] = both
            else:
                send_c[p] = both
                give_z(p).start()

    def tile(r, c):
        rows, cols = slice(*ROWS[r]), slice(*COLS[c])
        arg = dot(xa[rows, 0:128], ya[cols, 0:128], NT)
        adjoint = dot(xa[rows, 128:256], ya[cols, 128:256], NT)
        weighted = (adjoint * jnp.exp(arg)).astype(bf16)
        pulls = dot(weighted, ya[cols, 0:128], NN)
        rp[rows, :] = pulls if TILES.index((r, c)) == min(TILES.index((r, b)) for b in range(3)) else rp[rows, :] + pulls
        pulls = dot(xt[0:80, rows], weighted, NN)
        cp[0:80, cols] = pulls if r == 0 else cp[0:80, cols] + pulls

    arrive_z(1)
    arrive_z(2)
    arrive_x(near, 0, 12 * H)
    send_later()
    arrive_y(0, 1, 2)
    tile(0, 0)
    arrive_z(3)
    arrive_z(4)
    send_far()
    arrive_y(3, 4)
    tile(0, 1)
    arrive_x(later, 12 * H, 24 * H)
    tile(1, 0)
    arrive_z(5)
    arrive_z(6)
    tile(1, 1)
    arrive_z(7)
    arrive_y(5, 6, 7)
    tile(0, 2)
    finish_rows(0, 10)
    tile(1, 2)
    finish_rows(10, 24)
    arrive_x(far, 24 * H, 32 * H)
    tile(2, 2)
    finish_cols(5, 6, 7)
    tile(2, 1)
    finish_cols(3, 4)
    combine_cols(5, 6, 7)
    tile(2, 0)
    finish_cols(0, 1, 2)
    finish_rows(24, 32)
    combine_cols(3, 4)
    combine_cols(0, 1, 2)

    for h, k, i in blocks:
        give_r(h, k, i).wait_recv()
    halves = []
    for h in range(2):
        slots = [slot for slot, block in enumerate(SLOTS) if block[0] == h]
        halves.append(sum(recv_r[slot].astype(f32) for slot in slots))
    quarter = H // 2
    unpack(jnp.concatenate(halves, axis=0), [(0, 0, 0), (quarter, 0, 1), (H, quarter, 0), (H + quarter, quarter, 1)], out_s)
    for p in range(1, GROUP // 2):
        give_z(p).wait_recv()
    unpack(sum(recv_c[p].astype(f32) for p in range(GROUP // 2)), [(0, 0, 0), (H, 0, 1)], out_t)
    for h, k, i in blocks:
        give_r(h, k, i).wait_send()
    for p in range(GROUP // 2):
        share(p).wait_send()
        give_pair(p).wait_send()
        if p > 0:
            give_z(p).wait_send()
        if 0 < p < 7:
            hop(p).wait_send()
    for half in range(2):
        hop(7, half).wait_send()
    for steps in near + later + far:
        step_x(*steps).wait_send()


def per_device(source_embed, target_embed, left_factor, right_factor):
    frames = GROUP * B
    vmem = pl.BlockSpec(memory_space=pltpu.VMEM)
    return pl.pallas_call(
        kernel,
        out_shape=(jax.ShapeDtypeStruct((E, B), f32),) * 2,
        in_specs=[pl.BlockSpec(memory_space=pltpu.HBM)] * 4,
        out_specs=(vmem,) * 2,
        scratch_shapes=[
            pltpu.VMEM((frames, LANES), bf16),
            pltpu.VMEM((frames, LANES), bf16),
            pltpu.VMEM((128, frames), bf16),
            pltpu.VMEM((frames, 128), f32),
            pltpu.VMEM((128, frames), f32),
            pltpu.VMEM((2 * E, B), bf16),
            [pltpu.VMEM((2, E, B), bf16), pltpu.VMEM((2, B, R), bf16)],
        ]
        + [pltpu.VMEM((2 * GROUP, H // 2, 128), bf16)] * 2
        + [pltpu.VMEM((GROUP // 2, H, 128), bf16)] * 5
        + [pltpu.SemaphoreType.DMA((4,))]
        + [pltpu.SemaphoreType.DMA((2 * GROUP,))] * 2
        + [pltpu.SemaphoreType.DMA((GROUP,))] * 4
        + [pltpu.SemaphoreType.DMA((2 * GROUP,))] * 2
        + [pltpu.SemaphoreType.DMA((GROUP,))] * 4,
        compiler_params=pltpu.CompilerParams(
            collective_id=0, has_side_effects=True, vmem_limit_bytes=56 << 20
        ),
        cost_estimate=pl.CostEstimate(
            flops=2 * frames * frames * (2 * E + 2 * E + R), bytes_accessed=1 << 18, transcendentals=frames * frames
        ),
    )(source_embed, target_embed, left_factor.T, right_factor.T)


def solution(mesh):
    spec = P(None, ("row", "col"))
    return jax.shard_map(
        per_device, mesh=mesh, in_specs=(spec,) * 4, out_specs=(spec,) * 2, check_vma=False
    )
```

```python
import functools

import jax
import jax.numpy as jnp
from jax import lax
from jax.experimental import pallas as pl
from jax.experimental.pallas import tpu as pltpu
from jax.sharding import PartitionSpec as P

MESH = pl.DeviceIdType.MESH
f32, bf16 = jnp.float32, jnp.bfloat16

E = 64
R = 128
B = 192
LANES = E + 64 + R
GROUP = 16
H = B // 2
ONE_X, ONE_Y = E + 3, E

RING = [0, 1, 3, 2]
SLOTS = [(h, 0, i) for h in range(2) for i in range(4)] + [(h, k, 0) for h in range(2) for k in (1, 2)]
SLOTS += [(h, k, i) for h in range(2) for k in (1, 2) for i in (1, 2, 3)] + [(h, 3, i) for h in range(2) for i in range(4)]
LINE = [0, 1, 7, 2, 6, 3, 5, 4]

ROWS = [(0, 1024), (1024, 2304), (2304, 3072)]
COLS = [(0, 1024), (1024, 1792), (1792, 3072)]
TILES = [(0, 0), (0, 1), (1, 0), (1, 1), (0, 2), (1, 2), (2, 2), (2, 1), (2, 0)]

NN = (((1,), (0,)), ((), ()))
NT = (((1,), (1,)), ((), ()))


def dot(a, b, dims):
    return lax.dot_general(a, b, dims, preferred_element_type=f32)


def prepare(embed_ref, factor_ref, first, rows_ref, places, stack):
    wide = embed_ref[...].astype(f32)
    half = -0.5 * jnp.sum(wide * wide, axis=0, keepdims=True)
    high = half.astype(bf16).astype(f32)
    middle = (half - high).astype(bf16).astype(f32)
    low = half - high - middle
    place = lax.broadcasted_iota(jnp.int32, (E, B), 0)
    norms, ones = (0, 3) if first else (3, 0)
    extra = jnp.where((place >= ones) & (place < ones + 3), 1.0, 0.0)
    for at, piece in enumerate((high, middle, low)):
        extra = jnp.where(place == norms + at, piece, extra)
    stack[0:E, :] = embed_ref[...]
    stack[E : 2 * E, :] = extra.astype(bf16)
    down = lax.broadcasted_iota(jnp.int32, (B, B), 0)
    along = lax.broadcasted_iota(jnp.int32, (B, B), 1)
    unit = jnp.where(down == along, 1.0, 0.0).astype(bf16)
    left_lanes = dot(unit, stack[...], NT).astype(bf16)
    for half, at in enumerate(places):
        rows_ref[at : at + H, 0 : 2 * E] = left_lanes[half * H : (half + 1) * H]
        rows_ref[at : at + H, 2 * E : LANES] = factor_ref[half * H : (half + 1) * H, :]


def pack(block):
    n = block.shape[0] // 2
    lane = lax.broadcasted_iota(jnp.int32, (n, 128), 1)
    return jnp.where(lane < E, block[0:n], pltpu.roll(block[n:], E, 1)).astype(bf16)


def unpack(total, runs, out_ref):
    tall = jnp.concatenate([total, jnp.zeros((128 - H, 128), f32)], axis=0).T
    size = B // len(runs)
    lane = lax.broadcasted_iota(jnp.int32, (E, 128), 1)
    for begin in (0, 128):
        piece = jnp.zeros((E, 128), f32)
        for at, row, half in runs:
            if at < begin + 128 and at + size > begin:
                moved = pltpu.roll(tall[half * E : (half + 1) * E, :], (at - begin - row) % 128, 1)
                inside = (lane >= at - begin) & (lane < at - begin + size)
                piece = jnp.where(inside, moved, piece)
        width = min(128, B - begin)
        out_ref[:, begin : begin + width] = piece[:, 0:width]


def kernel(source, target, left, right, out, xa, ya, xt, rp, cp, stack, own, send_r, recv_r, mine, theirs, given, send_c, recv_c, *sems):
    in_sems, gx_s, gx_r, gz_s, gz_r, gc_s, gc_r, rr_s, rr_r, rc_s, rc_r, rz_s, rz_r = sems
    row, col = lax.axis_index("row"), lax.axis_index("col")
    y, z, core = row // 2, col // 4, col % 2
    x = (col // 2) % 2 * 2 + row % 2
    own_embed, own_factor = own
    out_s, out_t = out.at[0], out.at[1]

    def device(x, y, z, core):
        return (y % 4 * 2 + x % 2, (z % 8 * 2 + x % 4 // 2) * 2 + core)

    def frames_of(h, k, i, sign):
        dx, dy = (RING[i], RING[k]) if h == 0 else (RING[k], RING[i])
        return device(x + sign * dx % 4, y + sign * dy % 4, z, core)

    line_owner = [device(x, y, z + 8 - dz, core) for dz in LINE]
    line_to = [device(x, y, z + dz, core) for dz in LINE]
    sibling = device(x, y, z, 1 - core)

    def copy(src, dst, send, recv, peer):
        return pltpu.make_async_remote_copy(
            src_ref=src, dst_ref=dst, send_sem=send, recv_sem=recv, device_id=peer, device_id_type=MESH
        )

    def place(h, k, i):
        return SLOTS.index((h, k, i)) * H

    def step_x(h, k, i, n=1):
        old = place(h, 0, i) if k else place(h, 0, 0)
        at = SLOTS.index((h, k, i))
        peer = frames_of(h, k, 0, 1) if k else frames_of(h, 0, i, 1)
        return copy(xa.at[pl.ds(old, n * H), :], xa.at[pl.ds(at * H, n * H), :], gx_s.at[at], gx_r.at[at], peer)

    def hop(p, half=None):
        if p < 5:
            old, at, size, peer = 0, 2 * p * B, B, line_to[p]
        elif p < 7:
            old, at, size, peer = 2 * (p - 2) * B, 2 * p * B, B, line_to[p - 4]
        else:
            off = half * H
            old, at, size, peer = 2 * (3 + half) * B + off, 2 * p * B + off, H, line_to[3 + half]
        sem = p + (half or 0)
        return copy(ya.at[pl.ds(old, size), :], ya.at[pl.ds(at, size), :], gz_s.at[sem], gz_r.at[sem], peer)

    def share(p):
        return copy(ya.at[pl.ds(2 * p * B, B), :], ya.at[pl.ds((2 * p + 1) * B, B), :], gc_s.at[p], gc_r.at[p], sibling)

    def give_r(h, k, i):
        slot = SLOTS.index((h, k, i))
        return copy(send_r.at[slot], recv_r.at[slot], rr_s.at[slot], rr_r.at[slot], frames_of(h, k, i, -1))

    def give_pair(p):
        return copy(given.at[p], theirs.at[p], rc_s.at[p], rc_r.at[p], sibling)

    def give_z(p):
        return copy(send_c.at[p], recv_c.at[p], rz_s.at[p], rz_r.at[p], line_owner[p])

    blocks = [block for block in SLOTS if block[1] or block[2]]
    near = [(h, 0, i) for i in range(1, 4) for h in range(2)] + [(h, k, 0) for h in range(2) for k in (1, 2)]
    later = [(h, k, 1, 3) for k in (1, 2) for h in range(2)]
    far = [(h, 3, 0, 4) for h in range(2)]
    reads = [
        pltpu.make_async_copy(src, dst, in_sems.at[n])
        for n, (src, dst) in enumerate(zip((target, right, source, left), (own_embed.at[0], own_factor.at[0], own_embed.at[1], own_factor.at[1])))
    ]
    for read in reads:
        read.start()
    barrier = pltpu.get_barrier_semaphore()
    greet = [frames_of(h, 0, i, 1) for h in range(2) for i in range(1, 4)] + line_to[1:5] + [sibling]
    for peer in greet:
        pl.semaphore_signal(barrier, inc=1, device_id=peer, device_id_type=MESH)
    for read in reads[:2]:
        read.wait()
    prepare(own_embed.at[0], own_factor.at[0], False, ya, (0, H), stack)
    for read in reads[2:]:
        read.wait()
    prepare(own_embed.at[1], own_factor.at[1], True, xa, (place(0, 0, 0), place(1, 0, 0)), stack)
    pl.semaphore_wait(barrier, len(greet))
    share(0).start()
    for p in (1, 2):
        hop(p).start()
    for block in near:
        step_x(*block).start()
    for p in (3, 4):
        hop(p).start()
    cp[80:128, :] = jnp.zeros((48, cp.shape[1]), f32)

    def arrive_x(blocks, begin, end):
        for block in blocks:
            step_x(*block).wait_recv()
        xt[:, begin:end] = xa[begin:end, 0:128].T

    def send_later():
        for steps in later:
            step_x(*steps).start()

    def send_far():
        for steps in far:
            step_x(*steps).start()

    def arrive_z(p):
        if p < 7:
            hop(p).wait_recv()
        else:
            hop(7, 0).wait_recv()
            hop(7, 1).wait_recv()
        if p in (3, 4):
            hop(p + 2).start()
            hop(7, p - 3).start()
        share(p).start()

    def arrive_y(*pairs):
        for p in pairs:
            share(p).wait_recv()

    def grads(pulls, mass, embeds):
        return pulls - pulls[:, mass : mass + 1] * embeds.astype(f32)

    def finish_rows(begin, end):
        at = slice(begin * H, end * H)
        part = grads(rp[at, :], ONE_Y, xa[at, 0:128])
        for slot in range(begin, end):
            packed = pack(part[(slot - begin) * H : (slot - begin + 1) * H])
            if SLOTS[slot] in blocks:
                send_r[slot] = packed
                give_r(*SLOTS[slot]).start()
            else:
                recv_r[slot] = packed

    def finish_cols(*pairs):
        begin, end = 2 * pairs[0] * B, 2 * (pairs[-1] + 1) * B
        part = grads(cp[:, begin:end].T, ONE_X, ya[begin:end, 0:128])
        for i, p in enumerate(pairs):
            given[p] = pack(part[(2 * i + 1) * B : (2 * i + 2) * B])
            give_pair(p).start()
            mine[p] = pack(part[2 * i * B : (2 * i + 1) * B])

    def combine_cols(*pairs):
        for p in pairs:
            give_pair(p).wait_recv()
            both = (mine[p].astype(f32) + theirs[p].astype(f32)).astype(bf16)
            if p == 0:
                recv_c[0] = both
            else:
                send_c[p] = both
                give_z(p).start()

    def tile(r, c):
        rows, cols = slice(*ROWS[r]), slice(*COLS[c])
        arg = dot(xa[rows, 0:128], ya[cols, 0:128], NT)
        adjoint = dot(xa[rows, 128:256], ya[cols, 128:256], NT)
        weighted = (adjoint * jnp.exp(arg)).astype(bf16)
        pulls = dot(weighted, ya[cols, 0:128], NN)
        rp[rows, :] = pulls if TILES.index((r, c)) == min(TILES.index((r, b)) for b in range(3)) else rp[rows, :] + pulls
        pulls = dot(xt[0:80, rows], weighted, NN)
        cp[0:80, cols] = pulls if r == 0 else cp[0:80, cols] + pulls

    arrive_z(1)
    arrive_z(2)
    arrive_x(near, 0, 12 * H)
    send_later()
    arrive_y(0, 1, 2)
    tile(0, 0)
    arrive_z(3)
    arrive_z(4)
    send_far()
    arrive_y(3, 4)
    tile(0, 1)
    arrive_x(later, 12 * H, 24 * H)
    tile(1, 0)
    arrive_z(5)
    arrive_z(6)
    tile(1, 1)
    arrive_z(7)
    arrive_y(5, 6, 7)
    tile(0, 2)
    finish_rows(0, 10)
    tile(1, 2)
    finish_rows(10, 24)
    arrive_x(far, 24 * H, 32 * H)
    tile(2, 2)
    finish_cols(5, 6, 7)
    tile(2, 1)
    finish_cols(3, 4)
    combine_cols(5, 6, 7)
    tile(2, 0)
    finish_cols(0, 1, 2)
    finish_rows(24, 32)
    combine_cols(3, 4)
    combine_cols(0, 1, 2)

    for h, k, i in blocks:
        give_r(h, k, i).wait_recv()
    halves = []
    for h in range(2):
        slots = [slot for slot, block in enumerate(SLOTS) if block[0] == h]
        halves.append(sum(recv_r[slot].astype(f32) for slot in slots))
    quarter = H // 2
    unpack(jnp.concatenate(halves, axis=0), [(0, 0, 0), (quarter, 0, 1), (H, quarter, 0), (H + quarter, quarter, 1)], out_s)
    for p in range(1, GROUP // 2):
        give_z(p).wait_recv()
    unpack(sum(recv_c[p].astype(f32) for p in range(GROUP // 2)), [(0, 0, 0), (H, 0, 1)], out_t)
    for h, k, i in blocks:
        give_r(h, k, i).wait_send()
    for p in range(GROUP // 2):
        share(p).wait_send()
        give_pair(p).wait_send()
        if p > 0:
            give_z(p).wait_send()
        if 0 < p < 7:
            hop(p).wait_send()
    for half in range(2):
        hop(7, half).wait_send()
    for steps in near + later + far:
        step_x(*steps).wait_send()


def per_device(source_embed, target_embed, left_factor, right_factor):
    frames = GROUP * B
    vmem = pl.BlockSpec(memory_space=pltpu.VMEM)
    both = pl.pallas_call(
        kernel,
        out_shape=jax.ShapeDtypeStruct((2, E, B), f32),
        in_specs=[pl.BlockSpec(memory_space=pltpu.HBM)] * 4,
        out_specs=vmem,
        scratch_shapes=[
            pltpu.VMEM((frames, LANES), bf16),
            pltpu.VMEM((frames, LANES), bf16),
            pltpu.VMEM((128, frames), bf16),
            pltpu.VMEM((frames, 128), f32),
            pltpu.VMEM((128, frames), f32),
            pltpu.VMEM((2 * E, B), bf16),
            [pltpu.VMEM((2, E, B), bf16), pltpu.VMEM((2, B, R), bf16)],
        ]
        + [pltpu.VMEM((2 * GROUP, H // 2, 128), bf16)] * 2
        + [pltpu.VMEM((GROUP // 2, H, 128), bf16)] * 5
        + [pltpu.SemaphoreType.DMA((4,))]
        + [pltpu.SemaphoreType.DMA((2 * GROUP,))] * 2
        + [pltpu.SemaphoreType.DMA((GROUP,))] * 4
        + [pltpu.SemaphoreType.DMA((2 * GROUP,))] * 2
        + [pltpu.SemaphoreType.DMA((GROUP,))] * 4,
        compiler_params=pltpu.CompilerParams(
            collective_id=0, has_side_effects=True, vmem_limit_bytes=56 << 20
        ),
        cost_estimate=pl.CostEstimate(
            flops=2 * frames * frames * (2 * E + 2 * E + R), bytes_accessed=1 << 18, transcendentals=frames * frames
        ),
    )(source_embed, target_embed, left_factor.T, right_factor.T)
    return both[0], both[1]


def solution(mesh):
    spec = P(None, ("row", "col"))
    return jax.shard_map(
        per_device, mesh=mesh, in_specs=(spec,) * 4, out_specs=(spec,) * 2, check_vma=False
    )
```

```python
import functools

import jax
import jax.numpy as jnp
from jax import lax
from jax.experimental import pallas as pl
from jax.experimental.pallas import tpu as pltpu
from jax.sharding import PartitionSpec as P

MESH = pl.DeviceIdType.MESH
f32, bf16 = jnp.float32, jnp.bfloat16

E = 64
R = 128
B = 192
LANES = E + 64 + R
GROUP = 16
H = B // 2
ONE_X, ONE_Y = E + 3, E

RING = [0, 1, 3, 2]
SLOTS = [(h, 0, i) for h in range(2) for i in range(4)] + [(h, k, 0) for h in range(2) for k in (1, 2)]
SLOTS += [(h, k, i) for h in range(2) for k in (1, 2) for i in (1, 2, 3)] + [(h, 3, i) for h in range(2) for i in range(4)]
LINE = [0, 1, 7, 2, 6, 3, 5, 4]

ROWS = [(0, 1024), (1024, 2304), (2304, 3072)]
COLS = [(0, 1024), (1024, 1792), (1792, 3072)]
TILES = [(0, 0), (0, 1), (1, 0), (1, 1), (0, 2), (1, 2), (2, 2), (2, 1), (2, 0)]

NN = (((1,), (0,)), ((), ()))
NT = (((1,), (1,)), ((), ()))


def dot(a, b, dims):
    return lax.dot_general(a, b, dims, preferred_element_type=f32)


def prepare(embed_ref, factor_ref, first, rows_ref, places, stack):
    wide = embed_ref[...].astype(f32)
    half = -0.5 * jnp.sum(wide * wide, axis=0, keepdims=True)
    high = half.astype(bf16).astype(f32)
    middle = (half - high).astype(bf16).astype(f32)
    low = half - high - middle
    place = lax.broadcasted_iota(jnp.int32, (E, B), 0)
    norms, ones = (0, 3) if first else (3, 0)
    extra = jnp.where((place >= ones) & (place < ones + 3), 1.0, 0.0)
    for at, piece in enumerate((high, middle, low)):
        extra = jnp.where(place == norms + at, piece, extra)
    stack[0:E, :] = embed_ref[...]
    stack[E : 2 * E, :] = extra.astype(bf16)
    down = lax.broadcasted_iota(jnp.int32, (B, B), 0)
    along = lax.broadcasted_iota(jnp.int32, (B, B), 1)
    unit = jnp.where(down == along, 1.0, 0.0).astype(bf16)
    left_lanes = dot(unit, stack[...], NT).astype(bf16)
    for half, at in enumerate(places):
        rows_ref[at : at + H, 0 : 2 * E] = left_lanes[half * H : (half + 1) * H]
        rows_ref[at : at + H, 2 * E : LANES] = factor_ref[half * H : (half + 1) * H, :]


def pack(block):
    n = block.shape[0] // 2
    lane = lax.broadcasted_iota(jnp.int32, (n, 128), 1)
    return jnp.where(lane < E, block[0:n], pltpu.roll(block[n:], E, 1)).astype(bf16)


def unpack(total, runs, out_ref):
    tall = jnp.concatenate([total, jnp.zeros((128 - H, 128), f32)], axis=0).T
    size = B // len(runs)
    lane = lax.broadcasted_iota(jnp.int32, (E, 128), 1)
    for begin in (0, 128):
        piece = jnp.zeros((E, 128), f32)
        for at, row, half in runs:
            if at < begin + 128 and at + size > begin:
                moved = pltpu.roll(tall[half * E : (half + 1) * E, :], (at - begin - row) % 128, 1)
                inside = (lane >= at - begin) & (lane < at - begin + size)
                piece = jnp.where(inside, moved, piece)
        width = min(128, B - begin)
        out_ref[:, begin : begin + width] = piece[:, 0:width]


def kernel(source, target, left, right, out, xa, ya, xt, rp, cp, stack, own, send_r, recv_r, mine, theirs, given, send_c, recv_c, *sems):
    in_sems, gx_s, gx_r, gz_s, gz_r, gc_s, gc_r, rr_s, rr_r, rc_s, rc_r, rz_s, rz_r = sems
    row, col = lax.axis_index("row"), lax.axis_index("col")
    y, z, core = row // 2, col // 4, col % 2
    x = (col // 2) % 2 * 2 + row % 2
    own_embed, own_factor = own
    out_s, out_t = out.at[0], out.at[1]

    def device(x, y, z, core):
        return (y % 4 * 2 + x % 2, (z % 8 * 2 + x % 4 // 2) * 2 + core)

    def frames_of(h, k, i, sign):
        dx, dy = (RING[i], RING[k]) if h == 0 else (RING[k], RING[i])
        return device(x + sign * dx % 4, y + sign * dy % 4, z, core)

    line_owner = [device(x, y, z + 8 - dz, core) for dz in LINE]
    line_to = [device(x, y, z + dz, core) for dz in LINE]
    sibling = device(x, y, z, 1 - core)

    def copy(src, dst, send, recv, peer):
        return pltpu.make_async_remote_copy(
            src_ref=src, dst_ref=dst, send_sem=send, recv_sem=recv, device_id=peer, device_id_type=MESH
        )

    def place(h, k, i):
        return SLOTS.index((h, k, i)) * H

    def step_x(h, k, i, n=1):
        old = place(h, 0, i) if k else place(h, 0, 0)
        at = SLOTS.index((h, k, i))
        peer = frames_of(h, k, 0, 1) if k else frames_of(h, 0, i, 1)
        return copy(xa.at[pl.ds(old, n * H), :], xa.at[pl.ds(at * H, n * H), :], gx_s.at[at], gx_r.at[at], peer)

    def hop(p, half=None):
        if p < 5:
            old, at, size, peer = 0, 2 * p * B, B, line_to[p]
        elif p < 7:
            old, at, size, peer = 2 * (p - 2) * B, 2 * p * B, B, line_to[p - 4]
        else:
            off = half * H
            old, at, size, peer = 2 * (3 + half) * B + off, 2 * p * B + off, H, line_to[3 + half]
        sem = p + (half or 0)
        return copy(ya.at[pl.ds(old, size), :], ya.at[pl.ds(at, size), :], gz_s.at[sem], gz_r.at[sem], peer)

    def share(p):
        return copy(ya.at[pl.ds(2 * p * B, B), :], ya.at[pl.ds((2 * p + 1) * B, B), :], gc_s.at[p], gc_r.at[p], sibling)

    def give_r(h, k, i):
        slot = SLOTS.index((h, k, i))
        return copy(send_r.at[slot], recv_r.at[slot], rr_s.at[slot], rr_r.at[slot], frames_of(h, k, i, -1))

    def give_pair(p):
        return copy(given.at[p], theirs.at[p], rc_s.at[p], rc_r.at[p], sibling)

    def give_z(p):
        return copy(send_c.at[p], recv_c.at[p], rz_s.at[p], rz_r.at[p], line_owner[p])

    blocks = [block for block in SLOTS if block[1] or block[2]]
    near = [(h, 0, i) for i in range(1, 4) for h in range(2)] + [(h, k, 0) for h in range(2) for k in (1, 2)]
    later = [(h, k, 1, 3) for k in (1, 2) for h in range(2)]
    far = [(h, 3, 0, 4) for h in range(2)]
    reads = [
        pltpu.make_async_copy(src, dst, in_sems.at[n])
        for n, (src, dst) in enumerate(zip((target, right, source, left), (own_embed.at[0], own_factor.at[0], own_embed.at[1], own_factor.at[1])))
    ]
    for read in reads:
        read.start()
    barrier = pltpu.get_barrier_semaphore()
    greet = [frames_of(h, 0, i, 1) for h in range(2) for i in range(1, 4)] + line_to[1:5] + [sibling]
    for peer in greet:
        pl.semaphore_signal(barrier, inc=1, device_id=peer, device_id_type=MESH)
    for read in reads[:2]:
        read.wait()
    prepare(own_embed.at[0], own_factor.at[0], False, ya, (0, H), stack)
    for read in reads[2:]:
        read.wait()
    prepare(own_embed.at[1], own_factor.at[1], True, xa, (place(0, 0, 0), place(1, 0, 0)), stack)
    pl.semaphore_wait(barrier, len(greet))
    share(0).start()
    for p in (1, 2):
        hop(p).start()
    for block in near:
        step_x(*block).start()
    for p in (3, 4):
        hop(p).start()
    cp[80:128, :] = jnp.zeros((48, cp.shape[1]), f32)

    def arrive_x(blocks, begin, end):
        for block in blocks:
            step_x(*block).wait_recv()
        xt[:, begin:end] = xa[begin:end, 0:128].T

    def send_later():
        for steps in later:
            step_x(*steps).start()

    def send_far():
        for steps in far:
            step_x(*steps).start()

    def arrive_z(p):
        if p < 7:
            hop(p).wait_recv()
        else:
            hop(7, 0).wait_recv()
            hop(7, 1).wait_recv()
        if p in (3, 4):
            hop(p + 2).start()
            hop(7, p - 3).start()
        share(p).start()

    def arrive_y(*pairs):
        for p in pairs:
            share(p).wait_recv()

    def grads(pulls, mass, embeds):
        return pulls - pulls[:, mass : mass + 1] * embeds.astype(f32)

    def finish_rows(begin, end):
        at = slice(begin * H, end * H)
        part = grads(rp[at, :], ONE_Y, xa[at, 0:128])
        for slot in range(begin, end):
            packed = pack(part[(slot - begin) * H : (slot - begin + 1) * H])
            if SLOTS[slot] in blocks:
                send_r[slot] = packed
                give_r(*SLOTS[slot]).start()
            else:
                recv_r[slot] = packed

    def finish_cols(*pairs):
        begin, end = 2 * pairs[0] * B, 2 * (pairs[-1] + 1) * B
        part = grads(cp[:, begin:end].T, ONE_X, ya[begin:end, 0:128])
        for i, p in enumerate(pairs):
            given[p] = pack(part[(2 * i + 1) * B : (2 * i + 2) * B])
            give_pair(p).start()
            mine[p] = pack(part[2 * i * B : (2 * i + 1) * B])

    def combine_cols(*pairs):
        for p in pairs:
            give_pair(p).wait_recv()
            both = (mine[p].astype(f32) + theirs[p].astype(f32)).astype(bf16)
            if p == 0:
                recv_c[0] = both
            else:
                send_c[p] = both
                give_z(p).start()

    def tile(r, c):
        rows, cols = slice(*ROWS[r]), slice(*COLS[c])
        arg = dot(xa[rows, 0:128], ya[cols, 0:128], NT)
        adjoint = dot(xa[rows, 128:256], ya[cols, 128:256], NT)
        weighted = (adjoint * jnp.exp(arg)).astype(bf16)
        pulls = dot(weighted, ya[cols, 0:128], NN)
        rp[rows, :] = pulls if TILES.index((r, c)) == min(TILES.index((r, b)) for b in range(3)) else rp[rows, :] + pulls
        pulls = dot(xt[0:80, rows], weighted, NN)
        cp[0:80, cols] = pulls if r == 0 else cp[0:80, cols] + pulls

    arrive_z(1)
    arrive_z(2)
    arrive_x(near, 0, 12 * H)
    send_later()
    arrive_y(0, 1, 2)
    tile(0, 0)
    arrive_z(3)
    arrive_z(4)
    send_far()
    arrive_y(3, 4)
    tile(0, 1)
    arrive_x(later, 12 * H, 24 * H)
    tile(1, 0)
    arrive_z(5)
    arrive_z(6)
    tile(1, 1)
    arrive_z(7)
    arrive_y(5, 6, 7)
    tile(0, 2)
    finish_rows(0, 10)
    tile(1, 2)
    finish_rows(10, 24)
    arrive_x(far, 24 * H, 32 * H)
    tile(2, 2)
    finish_cols(5, 6, 7)
    tile(2, 1)
    finish_cols(3, 4)
    combine_cols(5, 6, 7)
    tile(2, 0)
    combine_cols(3, 4)
    finish_cols(0, 1, 2)
    finish_rows(24, 32)
    combine_cols(0, 1, 2)

    for h, k, i in blocks:
        give_r(h, k, i).wait_recv()
    halves = []
    for h in range(2):
        slots = [slot for slot, block in enumerate(SLOTS) if block[0] == h]
        halves.append(sum(recv_r[slot].astype(f32) for slot in slots))
    quarter = H // 2
    unpack(jnp.concatenate(halves, axis=0), [(0, 0, 0), (quarter, 0, 1), (H, quarter, 0), (H + quarter, quarter, 1)], out_s)
    for p in range(1, GROUP // 2):
        give_z(p).wait_recv()
    unpack(sum(recv_c[p].astype(f32) for p in range(GROUP // 2)), [(0, 0, 0), (H, 0, 1)], out_t)
    for h, k, i in blocks:
        give_r(h, k, i).wait_send()
    for p in range(GROUP // 2):
        share(p).wait_send()
        give_pair(p).wait_send()
        if p > 0:
            give_z(p).wait_send()
        if 0 < p < 7:
            hop(p).wait_send()
    for half in range(2):
        hop(7, half).wait_send()
    for steps in near + later + far:
        step_x(*steps).wait_send()


def per_device(source_embed, target_embed, left_factor, right_factor):
    frames = GROUP * B
    vmem = pl.BlockSpec(memory_space=pltpu.VMEM)
    both = pl.pallas_call(
        kernel,
        out_shape=jax.ShapeDtypeStruct((2, E, B), f32),
        in_specs=[pl.BlockSpec(memory_space=pltpu.HBM)] * 4,
        out_specs=vmem,
        scratch_shapes=[
            pltpu.VMEM((frames, LANES), bf16),
            pltpu.VMEM((frames, LANES), bf16),
            pltpu.VMEM((128, frames), bf16),
            pltpu.VMEM((frames, 128), f32),
            pltpu.VMEM((128, frames), f32),
            pltpu.VMEM((2 * E, B), bf16),
            [pltpu.VMEM((2, E, B), bf16), pltpu.VMEM((2, B, R), bf16)],
        ]
        + [pltpu.VMEM((2 * GROUP, H // 2, 128), bf16)] * 2
        + [pltpu.VMEM((GROUP // 2, H, 128), bf16)] * 5
        + [pltpu.SemaphoreType.DMA((4,))]
        + [pltpu.SemaphoreType.DMA((2 * GROUP,))] * 2
        + [pltpu.SemaphoreType.DMA((GROUP,))] * 4
        + [pltpu.SemaphoreType.DMA((2 * GROUP,))] * 2
        + [pltpu.SemaphoreType.DMA((GROUP,))] * 4,
        compiler_params=pltpu.CompilerParams(
            collective_id=0, has_side_effects=True, vmem_limit_bytes=56 << 20
        ),
        cost_estimate=pl.CostEstimate(
            flops=2 * frames * frames * (2 * E + 2 * E + R), bytes_accessed=1 << 18, transcendentals=frames * frames
        ),
    )(source_embed, target_embed, left_factor.T, right_factor.T)
    return both[0], both[1]


def solution(mesh):
    spec = P(None, ("row", "col"))
    return jax.shard_map(
        per_device, mesh=mesh, in_specs=(spec,) * 4, out_specs=(spec,) * 2, check_vma=False
    )
```
